32 devices in a mesh: wide: 8 (over z, y), lev: 4 (over x, core).
Axes of the slice: x: 2, y: 2, z: 4, core: 2. Of those that a mesh axis runs over, the one named last changes fastest.
Arguments:
- nonlinear: bfloat16 [3, 2, 256, 8, 4096], P(None, None, 'lev', None, 'wide'), may hold values from -20 to 20
Outputs:
- pressure: float32 [2, 256, 8, 1536], P(None, 'lev', 'wide')
The draws below stay inside these ranges and needn't reach their ends.
All inputs are finite; a program needn't handle non-finite values.
Results may differ from the reference program's by a relative error of at most 0.0034.
Values may be sent and summed in bfloat16 or wider, within the bound.
A program may use at most 64 MiB of HBM per device.

```python
import math
import jax
import jax.numpy as jnp
from jax import lax

NXG = 4096
KXM = 1536
NKY = 8
NZ = 256


def draw_nonlinear(key, part):
    keys = jax.random.split(key, 6)
    full_shape = (3, 2, NZ, NKY, NXG)
    white = jax.random.truncated_normal(keys[0], -4.0, 4.0, full_shape, jnp.float32)
    line = jax.random.truncated_normal(keys[1], -4.0, 4.0, (2, NKY, NXG), jnp.float32)
    level_gain = jax.random.uniform(keys[2], (2, 1, NKY, 1), jnp.float32, 2.0, 4.0)
    alternate_gain = jax.random.uniform(keys[3], (2, 1, NKY, 1), jnp.float32, -1.0, 1.0)
    phase = jax.random.uniform(keys[4], (2, 1, NKY, 1), jnp.float32, -math.pi, math.pi)
    cycles = jax.random.randint(keys[5], (2, 1, NKY, 1), 0, 3).astype(jnp.float32)
    level_index = jnp.arange(NZ, dtype=jnp.int32)
    levels = level_index.astype(jnp.float32)[None, :, None, None]
    signs = (1 - 2 * jnp.mod(level_index, 2)).astype(jnp.float32)[None, :, None, None]
    profile = level_gain * (1.0 + 0.5 * jnp.cos(2.0 * math.pi * cycles * levels / NZ + phase)) + alternate_gain * signs
    slope = line - jnp.roll(line, 1, axis=2)
    structured = profile * slope[:, None]
    first_field = white[0] + structured
    whole = jnp.concatenate([first_field[None], white[1:]], axis=0)
    return jnp.clip(whole, -20.0, 20.0).astype(jnp.bfloat16)


def setup_inputs(seed: int = 0) -> dict:
    key_list = jax.random.split(jax.random.key(seed), 2)
    return {
        "nonlinear": draw_nonlinear(jax.random.fold_in(key_list[1], 71), 0),
    }


def make_tables():
    places = jnp.arange(NXG, dtype=jnp.int32)
    waves = jnp.arange(KXM, dtype=jnp.int32) - KXM // 2
    phases = jnp.mod(places[:, None] * waves[None, :], NXG).astype(jnp.int32)
    angles = phases.astype(jnp.float32) * (2.0 * math.pi / NXG)
    return (jnp.cos(angles).astype(jnp.bfloat16), jnp.sin(angles).astype(jnp.bfloat16))

def wave_scales(first_row, row_count):
    spacing = 2.0 * math.pi / NXG
    ky_scaled = (first_row + jnp.arange(row_count, dtype=jnp.int32)).astype(jnp.float32) * spacing
    kx_scaled = (jnp.arange(KXM, dtype=jnp.int32) - KXM // 2).astype(jnp.float32) * spacing
    return (ky_scaled[:, None], kx_scaled[None, :])

def vertical_mix(y_term, z_padded, ky_scaled):
    upper = z_padded[:, 2:].astype(jnp.float32)
    lower = z_padded[:, :-2].astype(jnp.float32)
    half_diff = (upper - lower) * 0.5
    y_wide = y_term.astype(jnp.float32)
    real_part = half_diff[0] - ky_scaled * y_wide[1]
    imag_part = half_diff[1] + ky_scaled * y_wide[0]
    return jnp.stack([real_part, imag_part]).astype(jnp.bfloat16)

def spectral_source(x_term, g_term, cosine, sine, kx_scaled):
    stacked = jnp.concatenate([x_term, g_term], axis=0)
    lead_shape = stacked.shape[:3]
    flat_rows = stacked.reshape(-1, stacked.shape[3])
    with_cos = jnp.dot(flat_rows, cosine, preferred_element_type=jnp.float32).reshape(lead_shape + (cosine.shape[1],))
    with_sin = jnp.dot(flat_rows, sine, preferred_element_type=jnp.float32).reshape(lead_shape + (sine.shape[1],))
    norm_scale = 1.0 / math.sqrt(cosine.shape[0])
    fx_real = (with_cos[0] + with_sin[1]) * norm_scale
    fx_imag = (with_cos[1] - with_sin[0]) * norm_scale
    fg_real = (with_cos[2] + with_sin[3]) * norm_scale
    fg_imag = (with_cos[3] - with_sin[2]) * norm_scale
    return jnp.stack([kx_scaled * fx_imag - fg_real, -kx_scaled * fx_real - fg_imag])

def tridiag_sweep(diagonal, source):

    def forward_step(previous, row_data):
        shift_coef, prior_value = previous
        inverse = 1.0 / (diagonal + shift_coef)
        reduced_value = (row_data + prior_value) * inverse
        return ((-inverse, reduced_value), (inverse, reduced_value))
    initial = (jnp.zeros_like(diagonal), jnp.zeros_like(source[0]))
    _, (inverses, reduced) = lax.scan(forward_step, initial, source)

    def backward_step(following, row_pair):
        inverse, reduced_value = row_pair
        result = reduced_value + inverse * following
        return (result, result)
    _, solved = lax.scan(backward_step, jnp.zeros_like(source[0]), (inverses, reduced), reverse=True)
    return solved

def reference(nonlinear):
    cosine, sine = make_tables()
    ky_scaled, kx_scaled = wave_scales(0, NKY)
    field_x = nonlinear[0]
    field_y = nonlinear[1]
    padded = jnp.pad(nonlinear[2], ((0, 0), (1, 1), (0, 0), (0, 0)))

    def level_source(level):
        x_level = lax.dynamic_slice_in_dim(field_x, level, 1, 1)
        y_level = lax.dynamic_slice_in_dim(field_y, level, 1, 1)
        z_level = lax.dynamic_slice_in_dim(padded, level, 3, 1)
        combined = vertical_mix(y_level, z_level, ky_scaled)
        return spectral_source(x_level, combined, cosine, sine, kx_scaled)[:, 0]
    source = lax.map(level_source, jnp.arange(NZ, dtype=jnp.int32))
    diagonal = 2.0 + (ky_scaled * ky_scaled + kx_scaled * kx_scaled)
    solved = tridiag_sweep(diagonal, source)
    return jnp.moveaxis(solved, 0, 1)
```

```python
import functools
import math

import jax
import jax.numpy as jnp
import ml_dtypes
import numpy as np
from jax import lax
from jax.experimental import pallas as pl
from jax.experimental.pallas import tpu as pltpu
from jax.sharding import PartitionSpec as P

NXG = 4096
KXM = 1536
MESH = pl.DeviceIdType.MESH
COLS = 512


def make_tables():
    places = np.arange(NXG, dtype=np.int32)
    waves = np.arange(KXM, dtype=np.int32) - KXM // 2
    phases = np.mod(places[:, None] * waves[None, :], NXG)
    turn = np.arange(NXG, dtype=np.float32) * np.float32(2.0 * math.pi / NXG)
    cosine = np.cos(turn).astype(ml_dtypes.bfloat16)[phases]
    sine = np.sin(turn).astype(ml_dtypes.bfloat16)[phases]
    return np.concatenate([cosine, sine], axis=1)


def partner(me, step, count):
    total, unit = 0, 1
    while unit < count:
        total = total + unit * ((me // unit + step // unit) % 2)
        unit *= 2
    return total


def kernel(
    wide, lev, rows_ky, levels,
    x_ref, tab_ref, out_ref,
    tab, send, recv, halo_lo, halo_hi, zpad, acc, coef, from_lo, from_hi, part,
    ends, last_val, first_val,
    tab_sem, halo_send, halo_recv, send_sem, recv_sem, end_send, end_recv,
):
    chunk = x_ref.shape[3]
    line_rows = levels * rows_ky
    half = 2 * levels
    group_levels = max(16, 256 // rows_ky)
    group_rows = group_levels * rows_ky
    groups = levels // group_levels
    halo_rows = halo_lo.shape[1]
    me = lax.axis_index("wide")
    block = lax.axis_index("lev")

    tab_parts = tab_sem.shape[0]
    tab_rows = NXG // tab_parts

    def tab_copy(i):
        rows = pl.ds(i * tab_rows, tab_rows)
        return pltpu.make_async_copy(tab_ref.at[rows], tab.at[rows], tab_sem.at[i])

    barrier = pltpu.get_barrier_semaphore()
    for step in range(1, wide):
        pl.semaphore_signal(
            barrier, inc=1, device_id={"wide": partner(me, step, wide)}, device_id_type=MESH
        )
    for step in range(1, lev):
        pl.semaphore_signal(
            barrier, inc=1, device_id={"lev": (block + step) % lev}, device_id_type=MESH
        )
    pl.semaphore_wait(barrier, wide + lev - 2)

    to_prev = pltpu.make_async_remote_copy(
        src_ref=x_ref.at[2, :, 0:halo_rows],
        dst_ref=halo_hi,
        send_sem=halo_send.at[0],
        recv_sem=halo_recv.at[0],
        device_id={"lev": (block + lev - 1) % lev},
        device_id_type=MESH,
    )
    to_next = pltpu.make_async_remote_copy(
        src_ref=x_ref.at[2, :, line_rows - halo_rows:line_rows],
        dst_ref=halo_lo,
        send_sem=halo_send.at[1],
        recv_sem=halo_recv.at[1],
        device_id={"lev": (block + 1) % lev},
        device_id_type=MESH,
    )
    to_prev.start()
    to_next.start()

    out_row = lax.broadcasted_iota(jnp.int32, (group_rows, group_rows), 0)
    in_row = lax.broadcasted_iota(jnp.int32, (group_rows, group_rows), 1)
    wanted = (out_row % group_levels) * rows_ky + out_row // group_levels
    shuffle = jnp.where(in_row == wanted, 1.0, 0.0).astype(jnp.bfloat16)

    def place(values, first):
        moved = jnp.dot(shuffle, values, preferred_element_type=jnp.float32).astype(jnp.bfloat16)
        for ky in range(rows_ky):
            send[ky, first:first + group_levels, :] = moved[
                ky * group_levels:(ky + 1) * group_levels
            ]

    def line_copy(step, which):
        other = partner(me, step, wide)
        rows = pl.ds(which * half, half)
        return pltpu.make_async_remote_copy(
            src_ref=send.at[other, rows],
            dst_ref=recv.at[me, rows],
            send_sem=send_sem.at[which, step],
            recv_sem=recv_sem.at[which, step],
            device_id={"wide": other},
            device_id_type=MESH,
        )

    def line_arrival(step, which):
        other = partner(me, step, wide)
        rows = pl.ds(which * half, half)
        return pltpu.make_async_remote_copy(
            src_ref=send.at[other, rows],
            dst_ref=recv.at[other, rows],
            send_sem=send_sem.at[which, step],
            recv_sem=recv_sem.at[which, step],
            device_id={"wide": other},
            device_id_type=MESH,
        )

    for c in range(2):
        for g in range(groups):
            place(
                x_ref[0, c, g * group_rows:(g + 1) * group_rows, :],
                c * levels + g * group_levels,
            )
    for step in range(wide - 1, 0, -1):
        line_copy(step, 0).start()

    for i in range(tab_parts):
        tab_copy(i).start()

    for c in range(2):
        zpad[c, rows_ky:rows_ky + line_rows, :] = x_ref[2, c].astype(jnp.float32)
    to_prev.wait_recv()
    to_next.wait_recv()
    for c in range(2):
        low = halo_lo[c].astype(jnp.float32)[halo_rows - rows_ky:]
        high = halo_hi[c].astype(jnp.float32)[:rows_ky]
        zpad[c, 0:rows_ky, :] = jnp.where(block > 0, low, 0.0)
        zpad[c, rows_ky + line_rows:, :] = jnp.where(block < lev - 1, high, 0.0)
    spacing = 2.0 * math.pi / NXG
    ky_row = lax.broadcasted_iota(jnp.int32, (group_rows, chunk), 0) % rows_ky
    ky_scaled = ky_row.astype(jnp.float32) * spacing
    for c in range(2):
        for g in range(groups):
            at = g * group_rows
            upper = zpad[c, at + 2 * rows_ky:at + 2 * rows_ky + group_rows, :]
            lower = zpad[c, at:at + group_rows, :]
            turned = ky_scaled * x_ref[1, 1 - c, at:at + group_rows, :].astype(jnp.float32)
            slope = (upper - lower) * 0.5
            mixed = slope - turned if c == 0 else slope + turned
            place(mixed.astype(jnp.bfloat16), half + c * levels + g * group_levels)
    for step in range(wide - 1, 0, -1):
        line_copy(step, 1).start()

    kx_scaled = (
        lax.broadcasted_iota(jnp.int32, (1, KXM), 1) - KXM // 2
    ).astype(jnp.float32) * spacing
    ky_here = me.astype(jnp.float32) * spacing
    diagonal = 2.0 + (ky_here * ky_here + kx_scaled * kx_scaled)

    def coef_step(i, carry):
        shift, gain = carry
        inverse = 1.0 / (diagonal - shift)
        gain = gain * inverse
        coef[pl.ds(i, 1), :] = inverse
        from_lo[pl.ds(i, 1), :] = gain
        return inverse, gain

    zeros = jnp.zeros((1, KXM), jnp.float32)
    ones = jnp.ones((1, KXM), jnp.float32)
    lax.fori_loop(0, levels, coef_step, (zeros, ones))

    def unit_step(j, carry):
        i = levels - 1 - j
        low, high = carry
        inverse = coef[pl.ds(i, 1), :]
        low = from_lo[pl.ds(i, 1), :] + inverse * low
        high = inverse * high
        from_lo[pl.ds(i, 1), :] = low
        from_hi[pl.ds(i, 1), :] = high
        return low, high

    lax.fori_loop(0, levels, unit_step, (zeros, ones))

    for i in range(tab_parts):
        tab_copy(i).wait()

    own_at = pl.multiple_of(me * chunk, chunk)

    @pl.loop(0, 2 * KXM // COLS)
    def _(t):
        cols = pl.ds(pl.multiple_of(t * COLS, COLS), COLS)
        acc[:, cols] = jnp.dot(
            send[me], tab[pl.ds(own_at, chunk), cols], preferred_element_type=jnp.float32
        )

    def chunk_step(step, carry):
        line_arrival(step, 0).wait_recv()
        line_arrival(step, 1).wait_recv()
        other = partner(me, step, wide)
        rows = pl.ds(pl.multiple_of(other * chunk, chunk), chunk)

        @pl.loop(0, 2 * KXM // COLS)
        def _(t):
            cols = pl.ds(pl.multiple_of(t * COLS, COLS), COLS)
            acc[:, cols] += jnp.dot(
                recv[other], tab[rows, cols], preferred_element_type=jnp.float32
            )

        return carry

    lax.fori_loop(1, wide, chunk_step, 0)

    norm_scale = 1.0 / math.sqrt(NXG)

    @pl.loop(0, KXM // 256)
    def _(t):
        cc = pl.ds(pl.multiple_of(t * 256, 256), 256)
        ss = pl.ds(pl.multiple_of(KXM + t * 256, 256), 256)
        kx = (
            lax.broadcasted_iota(jnp.int32, (1, 256), 1) + t * 256 - KXM // 2
        ).astype(jnp.float32) * spacing
        n = levels
        fx_real = (acc[0:n, cc] + acc[n:2 * n, ss]) * norm_scale
        fx_imag = (acc[n:2 * n, cc] - acc[0:n, ss]) * norm_scale
        fg_real = (acc[2 * n:3 * n, cc] + acc[3 * n:4 * n, ss]) * norm_scale
        fg_imag = (acc[3 * n:4 * n, cc] - acc[2 * n:3 * n, ss]) * norm_scale
        part[0, :, cc] = kx * fx_imag - fg_real
        part[1, :, cc] = -kx * fx_real - fg_imag

    def down_step(i, carry):
        value = (part[:, pl.ds(i, 1), :] + carry) * coef[pl.ds(i, 1), :][None]
        part[:, pl.ds(i, 1), :] = value
        return value

    zero_pair = jnp.zeros((2, 1, KXM), jnp.float32)
    lax.fori_loop(0, levels, down_step, zero_pair, unroll=4)

    def up_step(j, carry):
        i = levels - 1 - j
        value = part[:, pl.ds(i, 1), :] + coef[pl.ds(i, 1), :][None] * carry
        part[:, pl.ds(i, 1), :] = value
        return value

    lax.fori_loop(0, levels, up_step, zero_pair, unroll=4)

    ends[block, 0:2, :] = part[:, 0, :]
    ends[block, 2:4, :] = part[:, levels - 1, :]

    def end_copy(step, slot):
        return pltpu.make_async_remote_copy(
            src_ref=ends.at[slot],
            dst_ref=ends.at[slot],
            send_sem=end_send.at[step],
            recv_sem=end_recv.at[step],
            device_id={"lev": (block + step) % lev},
            device_id_type=MESH,
        )

    for step in range(1, lev):
        end_copy(step, block).start()
    for step in range(1, lev):
        end_copy(step, (block + lev - step) % lev).wait_recv()

    near, far = from_lo[0:1, :], from_lo[levels - 1:levels, :]
    value, ratio = ends[0, 2:4, :], near
    values, ratios, inverses = [value], [ratio], [None]
    for b in range(1, lev):
        inverse = 1.0 / (1.0 - near * ratio)
        lead = far * ratio * inverse
        first = ends[b, 0:2, :] + near * value
        value = ends[b, 2:4, :] + far * value + lead * first
        ratio = near + lead * far
        values.append(value)
        ratios.append(ratio)
        inverses.append(inverse)
    follow = jnp.zeros((2, KXM), jnp.float32)
    first_val[lev] = follow
    last_val[0] = follow
    for b in range(lev - 1, 0, -1):
        follow = inverses[b] * (ends[b, 0:2, :] + near * values[b - 1] + far * follow)
        first_val[b] = follow
        last_val[b] = values[b - 1] + ratios[b - 1] * follow
    below = last_val[block]
    above = first_val[block + 1]
    for c in range(2):
        out_ref[c] = part[c] + from_lo[...] * below[c:c + 1] + from_hi[...] * above[c:c + 1]

    to_prev.wait_send()
    to_next.wait_send()
    for step in range(1, wide):
        line_copy(step, 0).wait_send()
        line_copy(step, 1).wait_send()
    for step in range(1, lev):
        end_copy(step, block).wait_send()


def solution(mesh):
    wide, lev = mesh.shape["wide"], mesh.shape["lev"]
    tables = make_tables()

    def local(nonlinear):
        _, _, levels, rows_ky, chunk = nonlinear.shape
        rows = levels * rows_ky
        halo_rows = max(16, rows_ky)
        f32, bf16 = jnp.float32, jnp.bfloat16
        dma = pltpu.SemaphoreType.DMA
        pressure = pl.pallas_call(
            functools.partial(kernel, wide, lev, rows_ky, levels),
            out_shape=jax.ShapeDtypeStruct((2, levels, KXM), f32),
            in_specs=[
                pl.BlockSpec(memory_space=pltpu.VMEM),
                pl.BlockSpec(memory_space=pl.ANY),
            ],
            out_specs=pl.BlockSpec(memory_space=pltpu.VMEM),
            scratch_shapes=[
                pltpu.VMEM((NXG, 2 * KXM), bf16),
                pltpu.VMEM((wide, 4 * levels, chunk), bf16),
                pltpu.VMEM((wide, 4 * levels, chunk), bf16),
                pltpu.VMEM((2, halo_rows, chunk), bf16),
                pltpu.VMEM((2, halo_rows, chunk), bf16),
                pltpu.VMEM((2, rows + 2 * rows_ky, chunk), f32),
                pltpu.VMEM((4 * levels, 2 * KXM), f32),
                pltpu.VMEM((levels, KXM), f32),
                pltpu.VMEM((levels, KXM), f32),
                pltpu.VMEM((levels, KXM), f32),
                pltpu.VMEM((2, levels, KXM), f32),
                pltpu.VMEM((lev, 8, KXM), f32),
                pltpu.VMEM((lev + 1, 2, KXM), f32),
                pltpu.VMEM((lev + 1, 2, KXM), f32),
                dma((8,)),
                dma((2,)),
                dma((2,)),
                dma((2, wide)),
                dma((2, wide)),
                dma((lev,)),
                dma((lev,)),
            ],
            compiler_params=pltpu.CompilerParams(
                collective_id=0, has_side_effects=True, vmem_limit_bytes=56 * 2**20
            ),
            cost_estimate=pl.CostEstimate(
                flops=2 * 4 * levels * NXG * 2 * KXM,
                bytes_accessed=NXG * 2 * KXM * 2 + 4 * rows * chunk * 2,
                transcendentals=0,
            ),
        )(nonlinear.reshape(3, 2, rows, chunk), jnp.asarray(tables))
        return pressure.reshape(2, levels, 1, KXM)

    placed = (P(None, None, "lev", None, "wide"),)
    return jax.shard_map(
        local, mesh=mesh, in_specs=placed, out_specs=P(None, "lev", "wide", None), check_vma=False
    )
```

```python
import functools
import math

import jax
import jax.numpy as jnp
import ml_dtypes
import numpy as np
from jax import lax
from jax.experimental import pallas as pl
from jax.experimental.pallas import tpu as pltpu
from jax.sharding import PartitionSpec as P

NXG = 4096
KXM = 1536
MESH = pl.DeviceIdType.MESH
COLS = 512


def make_tables():
    places = np.arange(NXG, dtype=np.int32)
    waves = np.arange(KXM, dtype=np.int32) - KXM // 2
    phases = np.mod(places[:, None] * waves[None, :], NXG)
    turn = np.arange(NXG, dtype=np.float32) * np.float32(2.0 * math.pi / NXG)
    cosine = np.cos(turn).astype(ml_dtypes.bfloat16)[phases]
    sine = np.sin(turn).astype(ml_dtypes.bfloat16)[phases]
    return np.concatenate([cosine, sine], axis=1)


def partner(me, step, count):
    total, unit = 0, 1
    while unit < count:
        total = total + unit * ((me // unit + step // unit) % 2)
        unit *= 2
    return total


def kernel(
    wide, lev, rows_ky, levels,
    x_ref, tab_ref, out_ref,
    tab, send, recv, halo_lo, halo_hi, zpad, acc, coef, from_lo, from_hi, part,
    ends, last_val, first_val,
    tab_sem, halo_send, halo_recv, send_sem, recv_sem, end_send, end_recv,
):
    chunk = x_ref.shape[3]
    line_rows = levels * rows_ky
    half = 2 * levels
    group_levels = max(16, 256 // rows_ky)
    group_rows = group_levels * rows_ky
    groups = levels // group_levels
    halo_rows = halo_lo.shape[1]
    me = lax.axis_index("wide")
    block = lax.axis_index("lev")

    tab_parts = tab_sem.shape[0]
    tab_rows = NXG // tab_parts

    def tab_copy(i):
        rows = pl.ds(i * tab_rows, tab_rows)
        return pltpu.make_async_copy(tab_ref.at[rows], tab.at[rows], tab_sem.at[i])

    barrier = pltpu.get_barrier_semaphore()
    for step in range(1, wide):
        pl.semaphore_signal(
            barrier, inc=1, device_id={"wide": partner(me, step, wide)}, device_id_type=MESH
        )
    for step in range(1, lev):
        pl.semaphore_signal(
            barrier, inc=1, device_id={"lev": (block + step) % lev}, device_id_type=MESH
        )
    out_row = lax.broadcasted_iota(jnp.int32, (group_rows, group_rows), 0)
    in_row = lax.broadcasted_iota(jnp.int32, (group_rows, group_rows), 1)
    wanted = (out_row % group_levels) * rows_ky + out_row // group_levels
    shuffle = jnp.where(in_row == wanted, 1.0, 0.0).astype(jnp.bfloat16)

    def place(values, first):
        moved = jnp.dot(shuffle, values, preferred_element_type=jnp.float32).astype(jnp.bfloat16)
        for ky in range(rows_ky):
            send[ky, first:first + group_levels, :] = moved[
                ky * group_levels:(ky + 1) * group_levels
            ]

    def line_copy(step, which):
        other = partner(me, step, wide)
        rows = pl.ds(which * half, half)
        return pltpu.make_async_remote_copy(
            src_ref=send.at[other, rows],
            dst_ref=recv.at[me, rows],
            send_sem=send_sem.at[which, step],
            recv_sem=recv_sem.at[which, step],
            device_id={"wide": other},
            device_id_type=MESH,
        )

    def line_arrival(step, which):
        other = partner(me, step, wide)
        rows = pl.ds(which * half, half)
        return pltpu.make_async_remote_copy(
            src_ref=send.at[other, rows],
            dst_ref=recv.at[other, rows],
            send_sem=send_sem.at[which, step],
            recv_sem=recv_sem.at[which, step],
            device_id={"wide": other},
            device_id_type=MESH,
        )

    for c in range(2):
        for g in range(groups):
            place(
                x_ref[0, c, g * group_rows:(g + 1) * group_rows, :],
                c * levels + g * group_levels,
            )
    pl.semaphore_wait(barrier, wide + lev - 2)

    to_prev = pltpu.make_async_remote_copy(
        src_ref=x_ref.at[2, :, 0:halo_rows],
        dst_ref=halo_hi,
        send_sem=halo_send.at[0],
        recv_sem=halo_recv.at[0],
        device_id={"lev": (block + lev - 1) % lev},
        device_id_type=MESH,
    )
    to_next = pltpu.make_async_remote_copy(
        src_ref=x_ref.at[2, :, line_rows - halo_rows:line_rows],
        dst_ref=halo_lo,
        send_sem=halo_send.at[1],
        recv_sem=halo_recv.at[1],
        device_id={"lev": (block + 1) % lev},
        device_id_type=MESH,
    )
    to_prev.start()
    to_next.start()

    far_steps = range(wide - 1, wide // 2 - 1, -1)
    near_steps = range(wide // 2 - 1, 0, -1)
    for step in far_steps:
        line_copy(step, 0).start()

    for i in range(tab_parts):
        tab_copy(i).start()

    for c in range(2):
        zpad[c, rows_ky:rows_ky + line_rows, :] = x_ref[2, c].astype(jnp.float32)
    to_prev.wait_recv()
    to_next.wait_recv()
    for c in range(2):
        low = halo_lo[c].astype(jnp.float32)[halo_rows - rows_ky:]
        high = halo_hi[c].astype(jnp.float32)[:rows_ky]
        zpad[c, 0:rows_ky, :] = jnp.where(block > 0, low, 0.0)
        zpad[c, rows_ky + line_rows:, :] = jnp.where(block < lev - 1, high, 0.0)
    spacing = 2.0 * math.pi / NXG
    ky_row = lax.broadcasted_iota(jnp.int32, (group_rows, chunk), 0) % rows_ky
    ky_scaled = ky_row.astype(jnp.float32) * spacing
    for c in range(2):
        for g in range(groups):
            at = g * group_rows
            upper = zpad[c, at + 2 * rows_ky:at + 2 * rows_ky + group_rows, :]
            lower = zpad[c, at:at + group_rows, :]
            turned = ky_scaled * x_ref[1, 1 - c, at:at + group_rows, :].astype(jnp.float32)
            slope = (upper - lower) * 0.5
            mixed = slope - turned if c == 0 else slope + turned
            place(mixed.astype(jnp.bfloat16), half + c * levels + g * group_levels)
    for step in far_steps:
        line_copy(step, 1).start()
    for step in near_steps:
        line_copy(step, 0).start()
        line_copy(step, 1).start()

    kx_scaled = (
        lax.broadcasted_iota(jnp.int32, (1, KXM), 1) - KXM // 2
    ).astype(jnp.float32) * spacing
    ky_here = me.astype(jnp.float32) * spacing
    diagonal = 2.0 + (ky_here * ky_here + kx_scaled * kx_scaled)

    def coef_step(i, carry):
        shift, gain = carry
        inverse = 1.0 / (diagonal - shift)
        gain = gain * inverse
        coef[pl.ds(i, 1), :] = inverse
        from_lo[pl.ds(i, 1), :] = gain
        return inverse, gain

    zeros = jnp.zeros((1, KXM), jnp.float32)
    ones = jnp.ones((1, KXM), jnp.float32)
    lax.fori_loop(0, levels, coef_step, (zeros, ones))

    def unit_step(j, carry):
        i = levels - 1 - j
        low, high = carry
        inverse = coef[pl.ds(i, 1), :]
        low = from_lo[pl.ds(i, 1), :] + inverse * low
        high = inverse * high
        from_lo[pl.ds(i, 1), :] = low
        from_hi[pl.ds(i, 1), :] = high
        return low, high

    lax.fori_loop(0, levels, unit_step, (zeros, ones))

    for i in range(tab_parts):
        tab_copy(i).wait()

    own_at = pl.multiple_of(me * chunk, chunk)

    @pl.loop(0, 2 * KXM // COLS)
    def _(t):
        cols = pl.ds(pl.multiple_of(t * COLS, COLS), COLS)
        acc[:, cols] = jnp.dot(
            send[me], tab[pl.ds(own_at, chunk), cols], preferred_element_type=jnp.float32
        )

    def chunk_step(step, carry):
        line_arrival(step, 0).wait_recv()
        line_arrival(step, 1).wait_recv()
        other = partner(me, step, wide)
        rows = pl.ds(pl.multiple_of(other * chunk, chunk), chunk)

        @pl.loop(0, 2 * KXM // COLS)
        def _(t):
            cols = pl.ds(pl.multiple_of(t * COLS, COLS), COLS)
            acc[:, cols] += jnp.dot(
                recv[other], tab[rows, cols], preferred_element_type=jnp.float32
            )

        return carry

    lax.fori_loop(1, wide - 1, chunk_step, 0)

    line_arrival(wide - 1, 0).wait_recv()
    line_arrival(wide - 1, 1).wait_recv()
    last = partner(me, wide - 1, wide)
    last_rows = pl.ds(pl.multiple_of(last * chunk, chunk), chunk)
    norm_scale = 1.0 / math.sqrt(NXG)

    @pl.loop(0, KXM // 256)
    def _(t):
        cc = pl.ds(pl.multiple_of(t * 256, 256), 256)
        ss = pl.ds(pl.multiple_of(KXM + t * 256, 256), 256)
        lines = recv[last]
        with_cos = acc[:, cc] + jnp.dot(
            lines, tab[last_rows, cc], preferred_element_type=jnp.float32
        )
        with_sin = acc[:, ss] + jnp.dot(
            lines, tab[last_rows, ss], preferred_element_type=jnp.float32
        )
        kx = (
            lax.broadcasted_iota(jnp.int32, (1, 256), 1) + t * 256 - KXM // 2
        ).astype(jnp.float32) * spacing
        n = levels
        fx_real = (with_cos[0:n] + with_sin[n:2 * n]) * norm_scale
        fx_imag = (with_cos[n:2 * n] - with_sin[0:n]) * norm_scale
        fg_real = (with_cos[2 * n:3 * n] + with_sin[3 * n:4 * n]) * norm_scale
        fg_imag = (with_cos[3 * n:4 * n] - with_sin[2 * n:3 * n]) * norm_scale
        source_real = kx * fx_imag - fg_real
        source_imag = -kx * fx_real - fg_imag
        part[0, :, cc] = source_real
        part[1, :, cc] = source_imag
        low, high = from_lo[:, cc], from_hi[:, cc]
        ends[block, 0:1, cc] = jnp.sum(low * source_real, axis=0, keepdims=True)
        ends[block, 1:2, cc] = jnp.sum(low * source_imag, axis=0, keepdims=True)
        ends[block, 2:3, cc] = jnp.sum(high * source_real, axis=0, keepdims=True)
        ends[block, 3:4, cc] = jnp.sum(high * source_imag, axis=0, keepdims=True)

    def end_copy(step, slot):
        return pltpu.make_async_remote_copy(
            src_ref=ends.at[slot],
            dst_ref=ends.at[slot],
            send_sem=end_send.at[step],
            recv_sem=end_recv.at[step],
            device_id={"lev": (block + step) % lev},
            device_id_type=MESH,
        )

    for step in range(1, lev):
        end_copy(step, block).start()

    def down_step(i, carry):
        value = (part[:, pl.ds(i, 1), :] + carry) * coef[pl.ds(i, 1), :][None]
        part[:, pl.ds(i, 1), :] = value
        return value

    zero_pair = jnp.zeros((2, 1, KXM), jnp.float32)
    lax.fori_loop(0, levels, down_step, zero_pair, unroll=4)

    def up_step(j, carry):
        i = levels - 1 - j
        value = part[:, pl.ds(i, 1), :] + coef[pl.ds(i, 1), :][None] * carry
        part[:, pl.ds(i, 1), :] = value
        return value

    lax.fori_loop(0, levels, up_step, zero_pair, unroll=4)

    for step in range(1, lev):
        end_copy(step, (block + lev - step) % lev).wait_recv()

    near, far = from_lo[0:1, :], from_lo[levels - 1:levels, :]
    value, ratio = ends[0, 2:4, :], near
    values, ratios, inverses = [value], [ratio], [None]
    for b in range(1, lev):
        inverse = 1.0 / (1.0 - near * ratio)
        lead = far * ratio * inverse
        first = ends[b, 0:2, :] + near * value
        value = ends[b, 2:4, :] + far * value + lead * first
        ratio = near + lead * far
        values.append(value)
        ratios.append(ratio)
        inverses.append(inverse)
    follow = jnp.zeros((2, KXM), jnp.float32)
    first_val[lev] = follow
    last_val[0] = follow
    for b in range(lev - 1, 0, -1):
        follow = inverses[b] * (ends[b, 0:2, :] + near * values[b - 1] + far * follow)
        first_val[b] = follow
        last_val[b] = values[b - 1] + ratios[b - 1] * follow
    below = last_val[block]
    above = first_val[block + 1]
    tiles = KXM // 128
    for c in range(2):
        for j in range(tiles):
            at = slice(j * 128, (j + 1) * 128)
            solved = (
                part[c, :, at]
                + from_lo[:, at] * below[c:c + 1, at]
                + from_hi[:, at] * above[c:c + 1, at]
            )
            out_ref[pl.ds(c * levels * tiles + j, levels, stride=tiles), :] = solved

    to_prev.wait_send()
    to_next.wait_send()
    for step in range(1, wide):
        line_copy(step, 0).wait_send()
        line_copy(step, 1).wait_send()
    for step in range(1, lev):
        end_copy(step, block).wait_send()


def solution(mesh):
    wide, lev = mesh.shape["wide"], mesh.shape["lev"]
    tables = make_tables()

    def local(nonlinear):
        _, _, levels, rows_ky, chunk = nonlinear.shape
        rows = levels * rows_ky
        halo_rows = max(16, rows_ky)
        f32, bf16 = jnp.float32, jnp.bfloat16
        dma = pltpu.SemaphoreType.DMA
        pressure = pl.pallas_call(
            functools.partial(kernel, wide, lev, rows_ky, levels),
            out_shape=jax.ShapeDtypeStruct((2 * levels * KXM // 128, 128), f32),
            in_specs=[
                pl.BlockSpec(memory_space=pltpu.VMEM),
                pl.BlockSpec(memory_space=pl.ANY),
            ],
            out_specs=pl.BlockSpec(memory_space=pltpu.VMEM),
            scratch_shapes=[
                pltpu.VMEM((NXG, 2 * KXM), bf16),
                pltpu.VMEM((wide, 4 * levels, chunk), bf16),
                pltpu.VMEM((wide, 4 * levels, chunk), bf16),
                pltpu.VMEM((2, halo_rows, chunk), bf16),
                pltpu.VMEM((2, halo_rows, chunk), bf16),
                pltpu.VMEM((2, rows + 2 * rows_ky, chunk), f32),
                pltpu.VMEM((4 * levels, 2 * KXM), f32),
                pltpu.VMEM((levels, KXM), f32),
                pltpu.VMEM((levels, KXM), f32),
                pltpu.VMEM((levels, KXM), f32),
                pltpu.VMEM((2, levels, KXM), f32),
                pltpu.VMEM((lev, 8, KXM), f32),
                pltpu.VMEM((lev + 1, 2, KXM), f32),
                pltpu.VMEM((lev + 1, 2, KXM), f32),
                dma((8,)),
                dma((2,)),
                dma((2,)),
                dma((2, wide)),
                dma((2, wide)),
                dma((lev,)),
                dma((lev,)),
            ],
            compiler_params=pltpu.CompilerParams(
                collective_id=0, has_side_effects=True, vmem_limit_bytes=56 * 2**20
            ),
            cost_estimate=pl.CostEstimate(
                flops=2 * 4 * levels * NXG * 2 * KXM,
                bytes_accessed=NXG * 2 * KXM * 2 + 4 * rows * chunk * 2,
                transcendentals=0,
            ),
        )(nonlinear.reshape(3, 2, rows, chunk), jnp.asarray(tables))
        return pressure.reshape(2, levels, 1, KXM)

    placed = (P(None, None, "lev", None, "wide"),)
    return jax.shard_map(
        local, mesh=mesh, in_specs=placed, out_specs=P(None, "lev", "wide", None), check_vma=False
    )
```

```python
import functools
import math

import jax
import jax.numpy as jnp
import ml_dtypes
import numpy as np
from jax import lax
from jax.experimental import pallas as pl
from jax.experimental.pallas import tpu as pltpu
from jax.sharding import PartitionSpec as P

NXG = 4096
KXM = 1536
MESH = pl.DeviceIdType.MESH
COLS = 512


def make_tables():
    places = np.arange(NXG, dtype=np.int32)
    waves = np.arange(KXM, dtype=np.int32) - KXM // 2
    phases = np.mod(places[:, None] * waves[None, :], NXG)
    turn = np.arange(NXG, dtype=np.float32) * np.float32(2.0 * math.pi / NXG)
    cosine = np.cos(turn).astype(ml_dtypes.bfloat16)[phases]
    sine = np.sin(turn).astype(ml_dtypes.bfloat16)[phases]
    return np.concatenate([cosine, sine], axis=1)


def partner(me, step, count):
    total, unit = 0, 1
    while unit < count:
        total = total + unit * ((me // unit + step // unit) % 2)
        unit *= 2
    return total


def kernel(
    wide, lev, rows_ky, levels,
    x_ref, tab_ref, out_ref,
    tab, send, recv, halo_lo, halo_hi, zpad, acc, coef, from_lo, from_hi, part, dense,
    ends, last_val, first_val,
    tab_sem, halo_send, halo_recv, send_sem, recv_sem, end_send, end_recv,
):
    chunk = x_ref.shape[3]
    line_rows = levels * rows_ky
    half = 2 * levels
    group_levels = max(16, 256 // rows_ky)
    group_rows = group_levels * rows_ky
    groups = levels // group_levels
    halo_rows = halo_lo.shape[1]
    me = lax.axis_index("wide")
    block = lax.axis_index("lev")

    tab_parts = tab_sem.shape[0]
    tab_rows = NXG // tab_parts

    def tab_copy(i):
        rows = pl.ds(i * tab_rows, tab_rows)
        return pltpu.make_async_copy(tab_ref.at[rows], tab.at[rows], tab_sem.at[i])

    barrier = pltpu.get_barrier_semaphore()
    for step in range(1, wide):
        pl.semaphore_signal(
            barrier, inc=1, device_id={"wide": partner(me, step, wide)}, device_id_type=MESH
        )
    for step in range(1, lev):
        pl.semaphore_signal(
            barrier, inc=1, device_id={"lev": (block + step) % lev}, device_id_type=MESH
        )
    out_row = lax.broadcasted_iota(jnp.int32, (group_rows, group_rows), 0)
    in_row = lax.broadcasted_iota(jnp.int32, (group_rows, group_rows), 1)
    wanted = (out_row % group_levels) * rows_ky + out_row // group_levels
    shuffle = jnp.where(in_row == wanted, 1.0, 0.0).astype(jnp.bfloat16)

    def place(values, first):
        moved = jnp.dot(shuffle, values, preferred_element_type=jnp.float32).astype(jnp.bfloat16)
        for ky in range(rows_ky):
            send[ky, first:first + group_levels, :] = moved[
                ky * group_levels:(ky + 1) * group_levels
            ]

    def line_copy(step, which):
        other = partner(me, step, wide)
        rows = pl.ds(which * half, half)
        return pltpu.make_async_remote_copy(
            src_ref=send.at[other, rows],
            dst_ref=recv.at[me, rows],
            send_sem=send_sem.at[which, step],
            recv_sem=recv_sem.at[which, step],
            device_id={"wide": other},
            device_id_type=MESH,
        )

    def line_arrival(step, which):
        other = partner(me, step, wide)
        rows = pl.ds(which * half, half)
        return pltpu.make_async_remote_copy(
            src_ref=send.at[other, rows],
            dst_ref=recv.at[other, rows],
            send_sem=send_sem.at[which, step],
            recv_sem=recv_sem.at[which, step],
            device_id={"wide": other},
            device_id_type=MESH,
        )

    for c in range(2):
        for g in range(groups):
            place(
                x_ref[0, c, g * group_rows:(g + 1) * group_rows, :],
                c * levels + g * group_levels,
            )
    pl.semaphore_wait(barrier, wide + lev - 2)

    to_prev = pltpu.make_async_remote_copy(
        src_ref=x_ref.at[2, :, 0:halo_rows],
        dst_ref=halo_hi,
        send_sem=halo_send.at[0],
        recv_sem=halo_recv.at[0],
        device_id={"lev": (block + lev - 1) % lev},
        device_id_type=MESH,
    )
    to_next = pltpu.make_async_remote_copy(
        src_ref=x_ref.at[2, :, line_rows - halo_rows:line_rows],
        dst_ref=halo_lo,
        send_sem=halo_send.at[1],
        recv_sem=halo_recv.at[1],
        device_id={"lev": (block + 1) % lev},
        device_id_type=MESH,
    )
    to_prev.start()
    to_next.start()

    quarter = wide // 4
    same = (me // (2 * quarter) + me // quarter + 1) % 2
    end_steps = [2 * quarter + same * quarter + i for i in range(quarter)]
    mid_steps = [2 * quarter + (1 - same) * quarter + i for i in range(quarter)]
    near_steps = range(wide // 2 - 1, 0, -1)
    for step in end_steps:
        line_copy(step, 0).start()

    for i in range(tab_parts):
        tab_copy(i).start()

    for c in range(2):
        zpad[c, rows_ky:rows_ky + line_rows, :] = x_ref[2, c].astype(jnp.float32)
    to_prev.wait_recv()
    to_next.wait_recv()
    for c in range(2):
        low = halo_lo[c].astype(jnp.float32)[halo_rows - rows_ky:]
        high = halo_hi[c].astype(jnp.float32)[:rows_ky]
        zpad[c, 0:rows_ky, :] = jnp.where(block > 0, low, 0.0)
        zpad[c, rows_ky + line_rows:, :] = jnp.where(block < lev - 1, high, 0.0)
    spacing = 2.0 * math.pi / NXG
    ky_row = lax.broadcasted_iota(jnp.int32, (group_rows, chunk), 0) % rows_ky
    ky_scaled = ky_row.astype(jnp.float32) * spacing
    for c in range(2):
        for g in range(groups):
            at = g * group_rows
            upper = zpad[c, at + 2 * rows_ky:at + 2 * rows_ky + group_rows, :]
            lower = zpad[c, at:at + group_rows, :]
            turned = ky_scaled * x_ref[1, 1 - c, at:at + group_rows, :].astype(jnp.float32)
            slope = (upper - lower) * 0.5
            mixed = slope - turned if c == 0 else slope + turned
            place(mixed.astype(jnp.bfloat16), half + c * levels + g * group_levels)
    for step in end_steps:
        line_copy(step, 1).start()
    for steps in (mid_steps, near_steps):
        for step in steps:
            line_copy(step, 0).start()
            line_copy(step, 1).start()

    kx_scaled = (
        lax.broadcasted_iota(jnp.int32, (1, KXM), 1) - KXM // 2
    ).astype(jnp.float32) * spacing
    ky_here = me.astype(jnp.float32) * spacing
    diagonal = 2.0 + (ky_here * ky_here + kx_scaled * kx_scaled)

    def coef_step(i, carry):
        shift, gain = carry
        inverse = 1.0 / (diagonal - shift)
        gain = gain * inverse
        coef[pl.ds(i, 1), :] = inverse
        from_lo[pl.ds(i, 1), :] = gain
        return inverse, gain

    zeros = jnp.zeros((1, KXM), jnp.float32)
    ones = jnp.ones((1, KXM), jnp.float32)
    lax.fori_loop(0, levels, coef_step, (zeros, ones))

    def unit_step(j, carry):
        i = levels - 1 - j
        low, high = carry
        inverse = coef[pl.ds(i, 1), :]
        low = from_lo[pl.ds(i, 1), :] + inverse * low
        high = inverse * high
        from_lo[pl.ds(i, 1), :] = low
        from_hi[pl.ds(i, 1), :] = high
        return low, high

    lax.fori_loop(0, levels, unit_step, (zeros, ones))

    tiles = KXM // 128
    deep = 2 * tiles
    for j in range(tiles):
        column = coef[:, j * 128:(j + 1) * 128]
        for c in range(2):
            dense[pl.ds(c * tiles + j, levels, stride=deep), :] = column

    for i in range(tab_parts):
        tab_copy(i).wait()

    own_at = pl.multiple_of(me * chunk, chunk)

    @pl.loop(0, 2 * KXM // COLS)
    def _(t):
        cols = pl.ds(pl.multiple_of(t * COLS, COLS), COLS)
        acc[:, cols] = jnp.dot(
            send[me], tab[pl.ds(own_at, chunk), cols], preferred_element_type=jnp.float32
        )

    def chunk_step(step, carry):
        line_arrival(step, 0).wait_recv()
        line_arrival(step, 1).wait_recv()
        other = partner(me, step, wide)
        rows = pl.ds(pl.multiple_of(other * chunk, chunk), chunk)

        @pl.loop(0, 2 * KXM // COLS)
        def _(t):
            cols = pl.ds(pl.multiple_of(t * COLS, COLS), COLS)
            acc[:, cols] += jnp.dot(
                recv[other], tab[rows, cols], preferred_element_type=jnp.float32
            )

        return carry

    lax.fori_loop(1, wide - 1, chunk_step, 0)

    line_arrival(wide - 1, 0).wait_recv()
    line_arrival(wide - 1, 1).wait_recv()
    last = partner(me, wide - 1, wide)
    last_rows = pl.ds(pl.multiple_of(last * chunk, chunk), chunk)
    norm_scale = 1.0 / math.sqrt(NXG)

    @pl.loop(0, KXM // 256)
    def _(t):
        cc = pl.ds(pl.multiple_of(t * 256, 256), 256)
        ss = pl.ds(pl.multiple_of(KXM + t * 256, 256), 256)
        lines = recv[last]
        with_cos = acc[:, cc] + jnp.dot(
            lines, tab[last_rows, cc], preferred_element_type=jnp.float32
        )
        with_sin = acc[:, ss] + jnp.dot(
            lines, tab[last_rows, ss], preferred_element_type=jnp.float32
        )
        kx = (
            lax.broadcasted_iota(jnp.int32, (1, 256), 1) + t * 256 - KXM // 2
        ).astype(jnp.float32) * spacing
        n = levels
        fx_real = (with_cos[0:n] + with_sin[n:2 * n]) * norm_scale
        fx_imag = (with_cos[n:2 * n] - with_sin[0:n]) * norm_scale
        fg_real = (with_cos[2 * n:3 * n] + with_sin[3 * n:4 * n]) * norm_scale
        fg_imag = (with_cos[3 * n:4 * n] - with_sin[2 * n:3 * n]) * norm_scale
        source_real = kx * fx_imag - fg_real
        source_imag = -kx * fx_real - fg_imag
        for j in range(2):
            at = slice(j * 128, (j + 1) * 128)
            part[pl.ds(2 * t + j, n, stride=deep), :] = source_real[:, at]
            part[pl.ds(tiles + 2 * t + j, n, stride=deep), :] = source_imag[:, at]
        low, high = from_lo[:, cc], from_hi[:, cc]
        ends[block, 0:1, cc] = jnp.sum(low * source_real, axis=0, keepdims=True)
        ends[block, 1:2, cc] = jnp.sum(low * source_imag, axis=0, keepdims=True)
        ends[block, 2:3, cc] = jnp.sum(high * source_real, axis=0, keepdims=True)
        ends[block, 3:4, cc] = jnp.sum(high * source_imag, axis=0, keepdims=True)

    def end_copy(step, slot):
        return pltpu.make_async_remote_copy(
            src_ref=ends.at[slot],
            dst_ref=ends.at[slot],
            send_sem=end_send.at[step],
            recv_sem=end_recv.at[step],
            device_id={"lev": (block + step) % lev},
            device_id_type=MESH,
        )

    for step in range(1, lev):
        end_copy(step, block).start()

    def down_step(i, carry):
        rows = pl.ds(pl.multiple_of(i * deep, 8), deep)
        value = (part[rows, :] + carry) * dense[rows, :]
        part[rows, :] = value
        return value

    zero_level = jnp.zeros((deep, 128), jnp.float32)
    lax.fori_loop(0, levels, down_step, zero_level, unroll=8)

    def up_step(j, carry):
        rows = pl.ds(pl.multiple_of((levels - 1 - j) * deep, 8), deep)
        value = part[rows, :] + dense[rows, :] * carry
        part[rows, :] = value
        return value

    lax.fori_loop(0, levels, up_step, zero_level, unroll=8)

    for step in range(1, lev):
        end_copy(step, (block + lev - step) % lev).wait_recv()

    near, far = from_lo[0:1, :], from_lo[levels - 1:levels, :]
    value, ratio = ends[0, 2:4, :], near
    values, ratios, inverses = [value], [ratio], [None]
    for b in range(1, lev):
        inverse = 1.0 / (1.0 - near * ratio)
        lead = far * ratio * inverse
        first = ends[b, 0:2, :] + near * value
        value = ends[b, 2:4, :] + far * value + lead * first
        ratio = near + lead * far
        values.append(value)
        ratios.append(ratio)
        inverses.append(inverse)
    follow = jnp.zeros((2, KXM), jnp.float32)
    first_val[lev] = follow
    last_val[0] = follow
    for b in range(lev - 1, 0, -1):
        follow = inverses[b] * (ends[b, 0:2, :] + near * values[b - 1] + far * follow)
        first_val[b] = follow
        last_val[b] = values[b - 1] + ratios[b - 1] * follow
    below = last_val[block]
    above = first_val[block + 1]
    for c in range(2):
        for j in range(tiles):
            at = slice(j * 128, (j + 1) * 128)
            solved = (
                part[pl.ds(c * tiles + j, levels, stride=deep), :]
                + from_lo[:, at] * below[c:c + 1, at]
                + from_hi[:, at] * above[c:c + 1, at]
            )
            out_ref[pl.ds(c * levels * tiles + j, levels, stride=tiles), :] = solved

    to_prev.wait_send()
    to_next.wait_send()
    for step in range(1, wide):
        line_copy(step, 0).wait_send()
        line_copy(step, 1).wait_send()
    for step in range(1, lev):
        end_copy(step, block).wait_send()


def solution(mesh):
    wide, lev = mesh.shape["wide"], mesh.shape["lev"]
    tables = make_tables()

    def local(nonlinear):
        _, _, levels, rows_ky, chunk = nonlinear.shape
        rows = levels * rows_ky
        halo_rows = max(16, rows_ky)
        f32, bf16 = jnp.float32, jnp.bfloat16
        dma = pltpu.SemaphoreType.DMA
        pressure = pl.pallas_call(
            functools.partial(kernel, wide, lev, rows_ky, levels),
            out_shape=jax.ShapeDtypeStruct((2 * levels * KXM // 128, 128), f32),
            in_specs=[
                pl.BlockSpec(memory_space=pltpu.VMEM),
                pl.BlockSpec(memory_space=pl.ANY),
            ],
            out_specs=pl.BlockSpec(memory_space=pltpu.VMEM),
            scratch_shapes=[
                pltpu.VMEM((NXG, 2 * KXM), bf16),
                pltpu.VMEM((wide, 4 * levels, chunk), bf16),
                pltpu.VMEM((wide, 4 * levels, chunk), bf16),
                pltpu.VMEM((2, halo_rows, chunk), bf16),
                pltpu.VMEM((2, halo_rows, chunk), bf16),
                pltpu.VMEM((2, rows + 2 * rows_ky, chunk), f32),
                pltpu.VMEM((4 * levels, 2 * KXM), f32),
                pltpu.VMEM((levels, KXM), f32),
                pltpu.VMEM((levels, KXM), f32),
                pltpu.VMEM((levels, KXM), f32),
                pltpu.VMEM((2 * levels * KXM // 128, 128), f32),
                pltpu.VMEM((2 * levels * KXM // 128, 128), f32),
                pltpu.VMEM((lev, 8, KXM), f32),
                pltpu.VMEM((lev + 1, 2, KXM), f32),
                pltpu.VMEM((lev + 1, 2, KXM), f32),
                dma((8,)),
                dma((2,)),
                dma((2,)),
                dma((2, wide)),
                dma((2, wide)),
                dma((lev,)),
                dma((lev,)),
            ],
            compiler_params=pltpu.CompilerParams(
                collective_id=0, has_side_effects=True, vmem_limit_bytes=56 * 2**20
            ),
            cost_estimate=pl.CostEstimate(
                flops=2 * 4 * levels * NXG * 2 * KXM,
                bytes_accessed=NXG * 2 * KXM * 2 + 4 * rows * chunk * 2,
                transcendentals=0,
            ),
        )(nonlinear.reshape(3, 2, rows, chunk), jnp.asarray(tables))
        return pressure.reshape(2, levels, 1, KXM)

    placed = (P(None, None, "lev", None, "wide"),)
    return jax.shard_map(
        local, mesh=mesh, in_specs=placed, out_specs=P(None, "lev", "wide", None), check_vma=False
    )
```

```python
import functools
import math

import jax
import jax.numpy as jnp
import ml_dtypes
import numpy as np
from jax import lax
from jax.experimental import pallas as pl
from jax.experimental.pallas import tpu as pltpu
from jax.sharding import PartitionSpec as P

NXG = 4096
KXM = 1536
MESH = pl.DeviceIdType.MESH
COLS = 512


def make_tables():
    places = np.arange(NXG, dtype=np.int32)
    waves = np.arange(KXM, dtype=np.int32) - KXM // 2
    phases = np.mod(places[:, None] * waves[None, :], NXG)
    turn = np.arange(NXG, dtype=np.float32) * np.float32(2.0 * math.pi / NXG)
    cosine = np.cos(turn).astype(ml_dtypes.bfloat16)[phases]
    sine = np.sin(turn).astype(ml_dtypes.bfloat16)[phases]
    return np.concatenate([cosine, sine], axis=1)


def partner(me, step, count):
    total, unit = 0, 1
    while unit < count:
        total = total + unit * ((me // unit + step // unit) % 2)
        unit *= 2
    return total


def kernel(
    wide, lev, rows_ky, levels,
    x_ref, tab_ref, out_ref,
    tab, send, recv, halo_lo, halo_hi, zpad, acc, coef, from_lo, from_hi, part, dense,
    ends, last_val, first_val,
    tab_sem, halo_send, halo_recv, send_sem, recv_sem, end_send, end_recv,
):
    chunk = x_ref.shape[3]
    line_rows = levels * rows_ky
    half = 2 * levels
    group_levels = max(16, 256 // rows_ky)
    group_rows = group_levels * rows_ky
    groups = levels // group_levels
    halo_rows = halo_lo.shape[1]
    me = lax.axis_index("wide")
    block = lax.axis_index("lev")

    tab_parts = tab_sem.shape[0]
    tab_rows = NXG // tab_parts

    def tab_copy(i):
        rows = pl.ds(i * tab_rows, tab_rows)
        return pltpu.make_async_copy(tab_ref.at[rows], tab.at[rows], tab_sem.at[i])

    barrier = pltpu.get_barrier_semaphore()
    for step in range(1, wide):
        pl.semaphore_signal(
            barrier, inc=1, device_id={"wide": partner(me, step, wide)}, device_id_type=MESH
        )
    for step in range(1, lev):
        pl.semaphore_signal(
            barrier, inc=1, device_id={"lev": (block + step) % lev}, device_id_type=MESH
        )
    out_row = lax.broadcasted_iota(jnp.int32, (group_rows, group_rows), 0)
    in_row = lax.broadcasted_iota(jnp.int32, (group_rows, group_rows), 1)
    wanted = (out_row % group_levels) * rows_ky + out_row // group_levels
    shuffle = jnp.where(in_row == wanted, 1.0, 0.0).astype(jnp.bfloat16)

    def place(values, first):
        moved = jnp.dot(shuffle, values, preferred_element_type=jnp.float32).astype(jnp.bfloat16)
        for ky in range(rows_ky):
            send[ky, first:first + group_levels, :] = moved[
                ky * group_levels:(ky + 1) * group_levels
            ]

    def line_copy(step, which):
        other = partner(me, step, wide)
        rows = pl.ds(which * half, half)
        return pltpu.make_async_remote_copy(
            src_ref=send.at[other, rows],
            dst_ref=recv.at[me, rows],
            send_sem=send_sem.at[which, step],
            recv_sem=recv_sem.at[which, step],
            device_id={"wide": other},
            device_id_type=MESH,
        )

    def line_arrival(step, which):
        other = partner(me, step, wide)
        rows = pl.ds(which * half, half)
        return pltpu.make_async_remote_copy(
            src_ref=send.at[other, rows],
            dst_ref=recv.at[other, rows],
            send_sem=send_sem.at[which, step],
            recv_sem=recv_sem.at[which, step],
            device_id={"wide": other},
            device_id_type=MESH,
        )

    for c in range(2):
        for g in range(groups):
            place(
                x_ref[0, c, g * group_rows:(g + 1) * group_rows, :],
                c * levels + g * group_levels,
            )
    pl.semaphore_wait(barrier, wide + lev - 2)

    to_prev = pltpu.make_async_remote_copy(
        src_ref=x_ref.at[2, :, 0:halo_rows],
        dst_ref=halo_hi,
        send_sem=halo_send.at[0],
        recv_sem=halo_recv.at[0],
        device_id={"lev": (block + lev - 1) % lev},
        device_id_type=MESH,
    )
    to_next = pltpu.make_async_remote_copy(
        src_ref=x_ref.at[2, :, line_rows - halo_rows:line_rows],
        dst_ref=halo_lo,
        send_sem=halo_send.at[1],
        recv_sem=halo_recv.at[1],
        device_id={"lev": (block + 1) % lev},
        device_id_type=MESH,
    )
    to_prev.start()
    to_next.start()

    quarter = wide // 4
    same = (me // (2 * quarter) + me // quarter + 1) % 2
    end_steps = [2 * quarter + same * quarter + i for i in range(quarter)]
    mid_steps = [2 * quarter + (1 - same) * quarter + i for i in range(quarter)]
    later_steps = []
    for i in range(wide // 2 - 1):
        later_steps.append(i + 1)
        if i < quarter:
            later_steps.append(mid_steps[i])
    for step in end_steps:
        line_copy(step, 0).start()

    for i in range(tab_parts):
        tab_copy(i).start()

    for c in range(2):
        zpad[c, rows_ky:rows_ky + line_rows, :] = x_ref[2, c].astype(jnp.float32)
    to_prev.wait_recv()
    to_next.wait_recv()
    for c in range(2):
        low = halo_lo[c].astype(jnp.float32)[halo_rows - rows_ky:]
        high = halo_hi[c].astype(jnp.float32)[:rows_ky]
        zpad[c, 0:rows_ky, :] = jnp.where(block > 0, low, 0.0)
        zpad[c, rows_ky + line_rows:, :] = jnp.where(block < lev - 1, high, 0.0)
    spacing = 2.0 * math.pi / NXG
    ky_row = lax.broadcasted_iota(jnp.int32, (group_rows, chunk), 0) % rows_ky
    ky_scaled = ky_row.astype(jnp.float32) * spacing
    for c in range(2):
        for g in range(groups):
            at = g * group_rows
            upper = zpad[c, at + 2 * rows_ky:at + 2 * rows_ky + group_rows, :]
            lower = zpad[c, at:at + group_rows, :]
            turned = ky_scaled * x_ref[1, 1 - c, at:at + group_rows, :].astype(jnp.float32)
            slope = (upper - lower) * 0.5
            mixed = slope - turned if c == 0 else slope + turned
            place(mixed.astype(jnp.bfloat16), half + c * levels + g * group_levels)
    for step in end_steps:
        line_copy(step, 1).start()
    for step in later_steps:
        line_copy(step, 0).start()
        line_copy(step, 1).start()

    kx_scaled = (
        lax.broadcasted_iota(jnp.int32, (1, KXM), 1) - KXM // 2
    ).astype(jnp.float32) * spacing
    ky_here = me.astype(jnp.float32) * spacing
    diagonal = 2.0 + (ky_here * ky_here + kx_scaled * kx_scaled)

    def coef_step(i, carry):
        shift, gain = carry
        inverse = 1.0 / (diagonal - shift)
        gain = gain * inverse
        coef[pl.ds(i, 1), :] = inverse
        from_lo[pl.ds(i, 1), :] = gain
        return inverse, gain

    zeros = jnp.zeros((1, KXM), jnp.float32)
    ones = jnp.ones((1, KXM), jnp.float32)
    lax.fori_loop(0, levels, coef_step, (zeros, ones))

    def unit_step(j, carry):
        i = levels - 1 - j
        low, high = carry
        inverse = coef[pl.ds(i, 1), :]
        low = from_lo[pl.ds(i, 1), :] + inverse * low
        high = inverse * high
        from_lo[pl.ds(i, 1), :] = low
        from_hi[pl.ds(i, 1), :] = high
        return low, high

    lax.fori_loop(0, levels, unit_step, (zeros, ones))

    tiles = KXM // 128
    deep = 2 * tiles
    for j in range(tiles):
        column = coef[:, j * 128:(j + 1) * 128]
        for c in range(2):
            dense[pl.ds(c * tiles + j, levels, stride=deep), :] = column

    for i in range(tab_parts):
        tab_copy(i).wait()

    own_at = pl.multiple_of(me * chunk, chunk)

    @pl.loop(0, 2 * KXM // COLS)
    def _(t):
        cols = pl.ds(pl.multiple_of(t * COLS, COLS), COLS)
        acc[:, cols] = jnp.dot(
            send[me], tab[pl.ds(own_at, chunk), cols], preferred_element_type=jnp.float32
        )

    def nth_step(n):
        return (n - 1 + same * (wide // 2 - 1)) % (wide - 1) + 1

    def chunk_step(n, carry):
        step = nth_step(n)
        line_arrival(step, 0).wait_recv()
        line_arrival(step, 1).wait_recv()
        other = partner(me, step, wide)
        rows = pl.ds(pl.multiple_of(other * chunk, chunk), chunk)

        @pl.loop(0, 2 * KXM // COLS)
        def _(t):
            cols = pl.ds(pl.multiple_of(t * COLS, COLS), COLS)
            acc[:, cols] += jnp.dot(
                recv[other], tab[rows, cols], preferred_element_type=jnp.float32
            )

        return carry

    lax.fori_loop(1, wide - 1, chunk_step, 0)

    last_step = nth_step(wide - 1)
    line_arrival(last_step, 0).wait_recv()
    line_arrival(last_step, 1).wait_recv()
    last = partner(me, last_step, wide)
    last_rows = pl.ds(pl.multiple_of(last * chunk, chunk), chunk)
    norm_scale = 1.0 / math.sqrt(NXG)

    @pl.loop(0, KXM // 256)
    def _(t):
        cc = pl.ds(pl.multiple_of(t * 256, 256), 256)
        ss = pl.ds(pl.multiple_of(KXM + t * 256, 256), 256)
        lines = recv[last]
        with_cos = acc[:, cc] + jnp.dot(
            lines, tab[last_rows, cc], preferred_element_type=jnp.float32
        )
        with_sin = acc[:, ss] + jnp.dot(
            lines, tab[last_rows, ss], preferred_element_type=jnp.float32
        )
        kx = (
            lax.broadcasted_iota(jnp.int32, (1, 256), 1) + t * 256 - KXM // 2
        ).astype(jnp.float32) * spacing
        n = levels
        fx_real = (with_cos[0:n] + with_sin[n:2 * n]) * norm_scale
        fx_imag = (with_cos[n:2 * n] - with_sin[0:n]) * norm_scale
        fg_real = (with_cos[2 * n:3 * n] + with_sin[3 * n:4 * n]) * norm_scale
        fg_imag = (with_cos[3 * n:4 * n] - with_sin[2 * n:3 * n]) * norm_scale
        source_real = kx * fx_imag - fg_real
        source_imag = -kx * fx_real - fg_imag
        for j in range(2):
            at = slice(j * 128, (j + 1) * 128)
            part[pl.ds(2 * t + j, n, stride=deep), :] = source_real[:, at]
            part[pl.ds(tiles + 2 * t + j, n, stride=deep), :] = source_imag[:, at]
        low, high = from_lo[:, cc], from_hi[:, cc]
        ends[block, 0:1, cc] = jnp.sum(low * source_real, axis=0, keepdims=True)
        ends[block, 1:2, cc] = jnp.sum(low * source_imag, axis=0, keepdims=True)
        ends[block, 2:3, cc] = jnp.sum(high * source_real, axis=0, keepdims=True)
        ends[block, 3:4, cc] = jnp.sum(high * source_imag, axis=0, keepdims=True)

    def end_copy(step, slot):
        return pltpu.make_async_remote_copy(
            src_ref=ends.at[slot],
            dst_ref=ends.at[slot],
            send_sem=end_send.at[step],
            recv_sem=end_recv.at[step],
            device_id={"lev": (block + step) % lev},
            device_id_type=MESH,
        )

    for step in range(1, lev):
        end_copy(step, block).start()

    def down_step(i, carry):
        rows = pl.ds(pl.multiple_of(i * deep, 8), deep)
        value = (part[rows, :] + carry) * dense[rows, :]
        part[rows, :] = value
        return value

    zero_level = jnp.zeros((deep, 128), jnp.float32)
    lax.fori_loop(0, levels, down_step, zero_level, unroll=8)

    def up_step(j, carry):
        rows = pl.ds(pl.multiple_of((levels - 1 - j) * deep, 8), deep)
        value = part[rows, :] + dense[rows, :] * carry
        part[rows, :] = value
        return value

    lax.fori_loop(0, levels, up_step, zero_level, unroll=8)

    for step in range(1, lev):
        end_copy(step, (block + lev - step) % lev).wait_recv()

    near, far = from_lo[0:1, :], from_lo[levels - 1:levels, :]
    value, ratio = ends[0, 2:4, :], near
    values, ratios, inverses = [value], [ratio], [None]
    for b in range(1, lev):
        inverse = 1.0 / (1.0 - near * ratio)
        lead = far * ratio * inverse
        first = ends[b, 0:2, :] + near * value
        value = ends[b, 2:4, :] + far * value + lead * first
        ratio = near + lead * far
        values.append(value)
        ratios.append(ratio)
        inverses.append(inverse)
    follow = jnp.zeros((2, KXM), jnp.float32)
    first_val[lev] = follow
    last_val[0] = follow
    for b in range(lev - 1, 0, -1):
        follow = inverses[b] * (ends[b, 0:2, :] + near * values[b - 1] + far * follow)
        first_val[b] = follow
        last_val[b] = values[b - 1] + ratios[b - 1] * follow
    below = last_val[block]
    above = first_val[block + 1]
    for c in range(2):
        for j in range(tiles):
            at = slice(j * 128, (j + 1) * 128)
            solved = (
                part[pl.ds(c * tiles + j, levels, stride=deep), :]
                + from_lo[:, at] * below[c:c + 1, at]
                + from_hi[:, at] * above[c:c + 1, at]
            )
            out_ref[pl.ds(c * levels * tiles + j, levels, stride=tiles), :] = solved

    to_prev.wait_send()
    to_next.wait_send()
    for step in range(1, wide):
        line_copy(step, 0).wait_send()
        line_copy(step, 1).wait_send()
    for step in range(1, lev):
        end_copy(step, block).wait_send()


def solution(mesh):
    wide, lev = mesh.shape["wide"], mesh.shape["lev"]
    tables = make_tables()

    def local(nonlinear):
        _, _, levels, rows_ky, chunk = nonlinear.shape
        rows = levels * rows_ky
        halo_rows = max(16, rows_ky)
        f32, bf16 = jnp.float32, jnp.bfloat16
        dma = pltpu.SemaphoreType.DMA
        pressure = pl.pallas_call(
            functools.partial(kernel, wide, lev, rows_ky, levels),
            out_shape=jax.ShapeDtypeStruct((2 * levels * KXM // 128, 128), f32),
            in_specs=[
                pl.BlockSpec(memory_space=pltpu.VMEM),
                pl.BlockSpec(memory_space=pl.ANY),
            ],
            out_specs=pl.BlockSpec(memory_space=pltpu.VMEM),
            scratch_shapes=[
                pltpu.VMEM((NXG, 2 * KXM), bf16),
                pltpu.VMEM((wide, 4 * levels, chunk), bf16),
                pltpu.VMEM((wide, 4 * levels, chunk), bf16),
                pltpu.VMEM((2, halo_rows, chunk), bf16),
                pltpu.VMEM((2, halo_rows, chunk), bf16),
                pltpu.VMEM((2, rows + 2 * rows_ky, chunk), f32),
                pltpu.VMEM((4 * levels, 2 * KXM), f32),
                pltpu.VMEM((levels, KXM), f32),
                pltpu.VMEM((levels, KXM), f32),
                pltpu.VMEM((levels, KXM), f32),
                pltpu.VMEM((2 * levels * KXM // 128, 128), f32),
                pltpu.VMEM((2 * levels * KXM // 128, 128), f32),
                pltpu.VMEM((lev, 8, KXM), f32),
                pltpu.VMEM((lev + 1, 2, KXM), f32),
                pltpu.VMEM((lev + 1, 2, KXM), f32),
                dma((8,)),
                dma((2,)),
                dma((2,)),
                dma((2, wide)),
                dma((2, wide)),
                dma((lev,)),
                dma((lev,)),
            ],
            compiler_params=pltpu.CompilerParams(
                collective_id=0, has_side_effects=True, vmem_limit_bytes=56 * 2**20
            ),
            cost_estimate=pl.CostEstimate(
                flops=2 * 4 * levels * NXG * 2 * KXM,
                bytes_accessed=NXG * 2 * KXM * 2 + 4 * rows * chunk * 2,
                transcendentals=0,
            ),
        )(nonlinear.reshape(3, 2, rows, chunk), jnp.asarray(tables))
        return pressure.reshape(2, levels, 1, KXM)

    placed = (P(None, None, "lev", None, "wide"),)
    return jax.shard_map(
        local, mesh=mesh, in_specs=placed, out_specs=P(None, "lev", "wide", None), check_vma=False
    )
```

```python
import functools
import math

import jax
import jax.numpy as jnp
import ml_dtypes
import numpy as np
from jax import lax
from jax.experimental import pallas as pl
from jax.experimental.pallas import tpu as pltpu
from jax.sharding import PartitionSpec as P

NXG = 4096
KXM = 1536
MESH = pl.DeviceIdType.MESH
COLS = 512


def make_tables():
    places = np.arange(NXG, dtype=np.int32)
    waves = np.arange(KXM, dtype=np.int32) - KXM // 2
    phases = np.mod(places[:, None] * waves[None, :], NXG)
    turn = np.arange(NXG, dtype=np.float32) * np.float32(2.0 * math.pi / NXG)
    cosine = np.cos(turn).astype(ml_dtypes.bfloat16)[phases]
    sine = np.sin(turn).astype(ml_dtypes.bfloat16)[phases]
    return np.concatenate([cosine, sine], axis=1)


def partner(me, step, count):
    total, unit = 0, 1
    while unit < count:
        total = total + unit * ((me // unit + step // unit) % 2)
        unit *= 2
    return total


def kernel(
    wide, lev, rows_ky, levels,
    x_ref, tab_ref, out_ref,
    tab, send, recv, halo_lo, halo_hi, zpad, acc, coef, from_lo, from_hi, part, dense,
    ends, last_val, first_val,
    tab_sem, halo_send, halo_recv, send_sem, recv_sem, end_send, end_recv,
):
    chunk = x_ref.shape[3]
    line_rows = levels * rows_ky
    half = 2 * levels
    group_levels = max(16, 256 // rows_ky)
    group_rows = group_levels * rows_ky
    groups = levels // group_levels
    halo_rows = halo_lo.shape[1]
    me = lax.axis_index("wide")
    block = lax.axis_index("lev")

    tab_parts = tab_sem.shape[0]
    tab_rows = NXG // tab_parts

    def tab_copy(i):
        rows = pl.ds(i * tab_rows, tab_rows)
        return pltpu.make_async_copy(tab_ref.at[rows], tab.at[rows], tab_sem.at[i])

    barrier = pltpu.get_barrier_semaphore()
    for step in range(1, wide):
        pl.semaphore_signal(
            barrier, inc=1, device_id={"wide": partner(me, step, wide)}, device_id_type=MESH
        )
    for step in range(1, lev):
        pl.semaphore_signal(
            barrier, inc=1, device_id={"lev": (block + step) % lev}, device_id_type=MESH
        )
    out_row = lax.broadcasted_iota(jnp.int32, (group_rows, group_rows), 0)
    in_row = lax.broadcasted_iota(jnp.int32, (group_rows, group_rows), 1)
    wanted = (out_row % group_levels) * rows_ky + out_row // group_levels
    shuffle = jnp.where(in_row == wanted, 1.0, 0.0).astype(jnp.bfloat16)

    def place(values, first):
        moved = jnp.dot(shuffle, values, preferred_element_type=jnp.float32).astype(jnp.bfloat16)
        for ky in range(rows_ky):
            send[ky, first:first + group_levels, :] = moved[
                ky * group_levels:(ky + 1) * group_levels
            ]

    def line_copy(step, which):
        other = partner(me, step, wide)
        rows = pl.ds(which * half, half)
        return pltpu.make_async_remote_copy(
            src_ref=send.at[other, rows],
            dst_ref=recv.at[me, rows],
            send_sem=send_sem.at[which, step],
            recv_sem=recv_sem.at[which, step],
            device_id={"wide": other},
            device_id_type=MESH,
        )

    def line_arrival(step, which):
        other = partner(me, step, wide)
        rows = pl.ds(which * half, half)
        return pltpu.make_async_remote_copy(
            src_ref=send.at[other, rows],
            dst_ref=recv.at[other, rows],
            send_sem=send_sem.at[which, step],
            recv_sem=recv_sem.at[which, step],
            device_id={"wide": other},
            device_id_type=MESH,
        )

    for c in range(2):
        for g in range(groups):
            place(
                x_ref[0, c, g * group_rows:(g + 1) * group_rows, :],
                c * levels + g * group_levels,
            )
    pl.semaphore_wait(barrier, wide + lev - 2)

    to_prev = pltpu.make_async_remote_copy(
        src_ref=x_ref.at[2, :, 0:halo_rows],
        dst_ref=halo_hi,
        send_sem=halo_send.at[0],
        recv_sem=halo_recv.at[0],
        device_id={"lev": (block + lev - 1) % lev},
        device_id_type=MESH,
    )
    to_next = pltpu.make_async_remote_copy(
        src_ref=x_ref.at[2, :, line_rows - halo_rows:line_rows],
        dst_ref=halo_lo,
        send_sem=halo_send.at[1],
        recv_sem=halo_recv.at[1],
        device_id={"lev": (block + 1) % lev},
        device_id_type=MESH,
    )
    to_prev.start()
    to_next.start()

    quarter = wide // 4
    same = (me // (2 * quarter) + me // quarter + 1) % 2
    end_steps = [2 * quarter + same * quarter + i for i in range(quarter)]
    mid_steps = [2 * quarter + (1 - same) * quarter + i for i in range(quarter)]
    near_steps = range(wide // 2 - 1, 0, -1)
    for step in end_steps:
        line_copy(step, 0).start()

    for i in range(tab_parts):
        tab_copy(i).start()

    for c in range(2):
        zpad[c, rows_ky:rows_ky + line_rows, :] = x_ref[2, c].astype(jnp.float32)
    to_prev.wait_recv()
    to_next.wait_recv()
    for c in range(2):
        low = halo_lo[c].astype(jnp.float32)[halo_rows - rows_ky:]
        high = halo_hi[c].astype(jnp.float32)[:rows_ky]
        zpad[c, 0:rows_ky, :] = jnp.where(block > 0, low, 0.0)
        zpad[c, rows_ky + line_rows:, :] = jnp.where(block < lev - 1, high, 0.0)
    spacing = 2.0 * math.pi / NXG
    ky_row = lax.broadcasted_iota(jnp.int32, (group_rows, chunk), 0) % rows_ky
    ky_scaled = ky_row.astype(jnp.float32) * spacing
    for c in range(2):
        for g in range(groups):
            at = g * group_rows
            upper = zpad[c, at + 2 * rows_ky:at + 2 * rows_ky + group_rows, :]
            lower = zpad[c, at:at + group_rows, :]
            turned = ky_scaled * x_ref[1, 1 - c, at:at + group_rows, :].astype(jnp.float32)
            slope = (upper - lower) * 0.5
            mixed = slope - turned if c == 0 else slope + turned
            place(mixed.astype(jnp.bfloat16), half + c * levels + g * group_levels)
    for step in end_steps:
        line_copy(step, 1).start()
    for steps in (mid_steps, near_steps):
        for step in steps:
            line_copy(step, 0).start()
            line_copy(step, 1).start()

    kx_scaled = (
        lax.broadcasted_iota(jnp.int32, (1, KXM), 1) - KXM // 2
    ).astype(jnp.float32) * spacing
    ky_here = me.astype(jnp.float32) * spacing
    diagonal = 2.0 + (ky_here * ky_here + kx_scaled * kx_scaled)

    def coef_step(i, carry):
        shift, gain = carry
        inverse = 1.0 / (diagonal - shift)
        gain = gain * inverse
        coef[pl.ds(i, 1), :] = inverse
        from_lo[pl.ds(i, 1), :] = gain
        return inverse, gain

    zeros = jnp.zeros((1, KXM), jnp.float32)
    ones = jnp.ones((1, KXM), jnp.float32)
    lax.fori_loop(0, levels, coef_step, (zeros, ones))

    def unit_step(j, carry):
        i = levels - 1 - j
        low, high = carry
        inverse = coef[pl.ds(i, 1), :]
        low = from_lo[pl.ds(i, 1), :] + inverse * low
        high = inverse * high
        from_lo[pl.ds(i, 1), :] = low
        from_hi[pl.ds(i, 1), :] = high
        return low, high

    lax.fori_loop(0, levels, unit_step, (zeros, ones))

    tiles = KXM // 128
    deep = 2 * tiles
    for j in range(tiles):
        column = coef[:, j * 128:(j + 1) * 128]
        for c in range(2):
            dense[pl.ds(c * tiles + j, levels, stride=deep), :] = column

    for i in range(tab_parts):
        tab_copy(i).wait()

    own_at = pl.multiple_of(me * chunk, chunk)

    @pl.loop(0, 2 * KXM // COLS)
    def _(t):
        cols = pl.ds(pl.multiple_of(t * COLS, COLS), COLS)
        acc[:, cols] = jnp.dot(
            send[me], tab[pl.ds(own_at, chunk), cols], preferred_element_type=jnp.float32
        )

    def chunk_step(step, carry):
        line_arrival(step, 0).wait_recv()
        line_arrival(step, 1).wait_recv()
        other = partner(me, step, wide)
        rows = pl.ds(pl.multiple_of(other * chunk, chunk), chunk)

        @pl.loop(0, 2 * KXM // COLS)
        def _(t):
            cols = pl.ds(pl.multiple_of(t * COLS, COLS), COLS)
            acc[:, cols] += jnp.dot(
                recv[other], tab[rows, cols], preferred_element_type=jnp.float32
            )

        return carry

    lax.fori_loop(1, wide - 1, chunk_step, 0)

    line_arrival(wide - 1, 0).wait_recv()
    line_arrival(wide - 1, 1).wait_recv()
    last = partner(me, wide - 1, wide)
    last_rows = pl.ds(pl.multiple_of(last * chunk, chunk), chunk)
    norm_scale = 1.0 / math.sqrt(NXG)

    @pl.loop(0, KXM // 256)
    def _(t):
        cc = pl.ds(pl.multiple_of(t * 256, 256), 256)
        ss = pl.ds(pl.multiple_of(KXM + t * 256, 256), 256)
        lines = recv[last]
        with_cos = acc[:, cc] + jnp.dot(
            lines, tab[last_rows, cc], preferred_element_type=jnp.float32
        )
        with_sin = acc[:, ss] + jnp.dot(
            lines, tab[last_rows, ss], preferred_element_type=jnp.float32
        )
        kx = (
            lax.broadcasted_iota(jnp.int32, (1, 256), 1) + t * 256 - KXM // 2
        ).astype(jnp.float32) * spacing
        n = levels
        fx_real = (with_cos[0:n] + with_sin[n:2 * n]) * norm_scale
        fx_imag = (with_cos[n:2 * n] - with_sin[0:n]) * norm_scale
        fg_real = (with_cos[2 * n:3 * n] + with_sin[3 * n:4 * n]) * norm_scale
        fg_imag = (with_cos[3 * n:4 * n] - with_sin[2 * n:3 * n]) * norm_scale
        source_real = kx * fx_imag - fg_real
        source_imag = -kx * fx_real - fg_imag
        for j in range(2):
            at = slice(j * 128, (j + 1) * 128)
            part[pl.ds(2 * t + j, n, stride=deep), :] = source_real[:, at]
            part[pl.ds(tiles + 2 * t + j, n, stride=deep), :] = source_imag[:, at]
        low, high = from_lo[:, cc], from_hi[:, cc]
        ends[block, 0:1, cc] = jnp.sum(low * source_real, axis=0, keepdims=True)
        ends[block, 1:2, cc] = jnp.sum(low * source_imag, axis=0, keepdims=True)
        ends[block, 2:3, cc] = jnp.sum(high * source_real, axis=0, keepdims=True)
        ends[block, 3:4, cc] = jnp.sum(high * source_imag, axis=0, keepdims=True)

    def end_copy(step, slot):
        return pltpu.make_async_remote_copy(
            src_ref=ends.at[slot],
            dst_ref=ends.at[slot],
            send_sem=end_send.at[step],
            recv_sem=end_recv.at[step],
            device_id={"lev": (block + step) % lev},
            device_id_type=MESH,
        )

    for step in range(1, lev):
        end_copy(step, block).start()

    def down_step(i, carry):
        rows = pl.ds(pl.multiple_of(i * deep, 8), deep)
        value = (part[rows, :] + carry) * dense[rows, :]
        part[rows, :] = value
        return value

    zero_level = jnp.zeros((deep, 128), jnp.float32)
    lax.fori_loop(0, levels, down_step, zero_level, unroll=8)

    def up_step(j, carry):
        rows = pl.ds(pl.multiple_of((levels - 1 - j) * deep, 8), deep)
        value = part[rows, :] + dense[rows, :] * carry
        part[rows, :] = value
        return value

    lax.fori_loop(0, levels, up_step, zero_level, unroll=8)

    for step in range(1, lev):
        end_copy(step, (block + lev - step) % lev).wait_recv()

    near, far = from_lo[0:1, :], from_lo[levels - 1:levels, :]
    value, ratio = ends[0, 2:4, :], near
    values, ratios, inverses = [value], [ratio], [None]
    for b in range(1, lev):
        inverse = 1.0 / (1.0 - near * ratio)
        lead = far * ratio * inverse
        first = ends[b, 0:2, :] + near * value
        value = ends[b, 2:4, :] + far * value + lead * first
        ratio = near + lead * far
        values.append(value)
        ratios.append(ratio)
        inverses.append(inverse)
    follow = jnp.zeros((2, KXM), jnp.float32)
    first_val[lev] = follow
    last_val[0] = follow
    for b in range(lev - 1, 0, -1):
        follow = inverses[b] * (ends[b, 0:2, :] + near * values[b - 1] + far * follow)
        first_val[b] = follow
        last_val[b] = values[b - 1] + ratios[b - 1] * follow
    below = last_val[block]
    above = first_val[block + 1]
    for c in range(2):
        for j in range(tiles):
            at = slice(j * 128, (j + 1) * 128)
            solved = (
                part[pl.ds(c * tiles + j, levels, stride=deep), :]
                + from_lo[:, at] * below[c:c + 1, at]
                + from_hi[:, at] * above[c:c + 1, at]
            )
            out_ref[pl.ds(c * levels * tiles + j, levels, stride=tiles), :] = solved

    to_prev.wait_send()
    to_next.wait_send()
    for step in range(1, wide):
        line_copy(step, 0).wait_send()
        line_copy(step, 1).wait_send()
    for step in range(1, lev):
        end_copy(step, block).wait_send()


def hand_over(x_ref, out_ref):
    out_ref[...] = x_ref[...]


def solution(mesh):
    wide, lev = mesh.shape["wide"], mesh.shape["lev"]
    tables = make_tables()

    def local(nonlinear):
        _, _, levels, rows_ky, chunk = nonlinear.shape
        rows = levels * rows_ky
        halo_rows = max(16, rows_ky)
        f32, bf16 = jnp.float32, jnp.bfloat16
        dma = pltpu.SemaphoreType.DMA
        pressure = pl.pallas_call(
            functools.partial(kernel, wide, lev, rows_ky, levels),
            out_shape=jax.ShapeDtypeStruct((2 * levels * KXM // 128, 128), f32),
            in_specs=[
                pl.BlockSpec(memory_space=pltpu.VMEM),
                pl.BlockSpec(memory_space=pl.ANY),
            ],
            out_specs=pl.BlockSpec(memory_space=pltpu.VMEM),
            scratch_shapes=[
                pltpu.VMEM((NXG, 2 * KXM), bf16),
                pltpu.VMEM((wide, 4 * levels, chunk), bf16),
                pltpu.VMEM((wide, 4 * levels, chunk), bf16),
                pltpu.VMEM((2, halo_rows, chunk), bf16),
                pltpu.VMEM((2, halo_rows, chunk), bf16),
                pltpu.VMEM((2, rows + 2 * rows_ky, chunk), f32),
                pltpu.VMEM((4 * levels, 2 * KXM), f32),
                pltpu.VMEM((levels, KXM), f32),
                pltpu.VMEM((levels, KXM), f32),
                pltpu.VMEM((levels, KXM), f32),
                pltpu.VMEM((2 * levels * KXM // 128, 128), f32),
                pltpu.VMEM((2 * levels * KXM // 128, 128), f32),
                pltpu.VMEM((lev, 8, KXM), f32),
                pltpu.VMEM((lev + 1, 2, KXM), f32),
                pltpu.VMEM((lev + 1, 2, KXM), f32),
                dma((8,)),
                dma((2,)),
                dma((2,)),
                dma((2, wide)),
                dma((2, wide)),
                dma((lev,)),
                dma((lev,)),
            ],
            compiler_params=pltpu.CompilerParams(
                collective_id=0, has_side_effects=True, vmem_limit_bytes=56 * 2**20
            ),
            cost_estimate=pl.CostEstimate(
                flops=2 * 4 * levels * NXG * 2 * KXM,
                bytes_accessed=NXG * 2 * KXM * 2 + 4 * rows * chunk * 2,
                transcendentals=0,
            ),
        )(nonlinear.reshape(3, 2, rows, chunk), jnp.asarray(tables))
        pressure = pl.pallas_call(
            hand_over, out_shape=jax.ShapeDtypeStruct(pressure.shape, f32)
        )(pressure)
        return pressure.reshape(2, levels, 1, KXM)

    placed = (P(None, None, "lev", None, "wide"),)
    return jax.shard_map(
        local, mesh=mesh, in_specs=placed, out_specs=P(None, "lev", "wide", None), check_vma=False
    )
```
